128 devices in a mesh: blk: 64 (over y, z_hi, x, core), rep: 2 (over z_lo).
Axes of the slice: x: 4, y: 4, z: 4 (z_hi: 2, z_lo: 2; z = z_hi * 2 + z_lo), core: 2. Of those that a mesh axis runs over, the one named last changes fastest.
Arguments:
- feature_codes: bfloat16 [32768, 512], P('blk', 'rep'), may hold values from -6 to 6
- group_scales: float32 [32768, 4], P('blk', 'rep'), may hold values from 0.25 to 2
- adjacency: bfloat16 [32768, 128, 128], P('blk'), may hold values from 0 to 2, as said below
- tile_source: int32 [32768], P('blk'), may hold values from 0 to 255, as said below
- tile_target: int32 [32768], P('blk'), may hold values from 0 to 3
- weight: bfloat16 [1024, 512], replicated, may hold values from -0.1875 to 0.1875
- out_bias: float32 [512], P('rep'), may hold values from -3 to 3
Outputs:
- hidden: bfloat16 [32768, 512], P('blk', 'rep')
The draws below stay inside these ranges and needn't reach their ends.
Inputs may be any that keep to these rules, and one draw needn't show every extreme that they name: Entries 512 b to 512 (b + 1) - 1 are block b's tiles, in ascending order of tile_source; no two tiles of one block share both source and target tile. `adjacency`: entries are 0 or positive.
All inputs are finite; a program needn't handle non-finite values.
Results may differ from the reference program's by a relative error of at most 0.0052.
Values may be sent and summed in bfloat16 or wider, within the bound.
No kernel may reach another device: no remote copies, remote signals or barrier semaphores. Data moves between devices by JAX's collectives and lax.ppermute only.
A program may use at most 128 MiB of HBM per device.

```python
import math
import jax
import jax.numpy as jnp
from jax import lax

F = 512
FO = 512
TILE = 128
GROUP = 128
NTD = 4
TILES_DEV = 512
ALL_TILES = 32768
NODES = 32768
N_BLK = 64


def chosen_pairs(key):
    pairs = N_BLK * NTD * NTD
    popular = jax.random.randint(jax.random.fold_in(key, 11), (N_BLK,), 0, 1024)
    pair_index = jnp.arange(pairs, dtype=jnp.int32)
    source_block = pair_index // (NTD * NTD)

    def one_block(block_id):
        jitter = jax.random.randint(jax.random.fold_in(key, 1000 + block_id), (pairs,), 0, 1024)
        ahead = (source_block - block_id) % N_BLK
        behind = (block_id - source_block) % N_BLK
        spacing = jnp.minimum(ahead, behind)
        nearby = jnp.where(spacing == 0, 30000, jnp.where(spacing == 1, 4096, jnp.maximum(0, 2048 - 128 * spacing)))
        ranking = (jitter + popular[source_block] + nearby) * pairs + pair_index
        top_values, picked = lax.top_k(ranking, TILES_DEV)
        return jnp.sort(picked).astype(jnp.int32)
    return lax.map(one_block, jnp.arange(N_BLK, dtype=jnp.int32)).reshape(-1)


def draw_tile_source(key, part):
    return (chosen_pairs(key) // NTD).astype(jnp.int32)


def draw_tile_target(key, part):
    return (chosen_pairs(key) % NTD).astype(jnp.int32)


def draw_adjacency(key, part):
    targets = (chosen_pairs(key) % NTD).reshape(N_BLK, TILES_DEV)
    key = jax.random.fold_in(key, 5)
    low_rate, high_rate, low_value, high_value = (0.04, 0.4, 0.5, 1.5)
    rates = jnp.exp(jax.random.uniform(jax.random.fold_in(key, 1), (N_BLK, NTD, TILE), jnp.float32, math.log(low_rate), math.log(high_rate)))

    def one_block(block_id):
        row_rate = jnp.take(rates[block_id], targets[block_id], axis=0)
        chance = jax.random.uniform(jax.random.fold_in(key, 2000 + block_id), (TILES_DEV, TILE, TILE), jnp.float32)
        values = jax.random.uniform(jax.random.fold_in(key, 5000 + block_id), (TILES_DEV, TILE, TILE), jnp.float32, low_value, high_value)
        return jnp.where(chance < row_rate[:, :, None], values, 0.0).astype(jnp.bfloat16)
    return lax.map(one_block, jnp.arange(N_BLK, dtype=jnp.int32)).reshape(ALL_TILES, TILE, TILE)


def steps_of(rng, extent, shards, low, high):
    def one(axis_at, shards_of):
        heights = jax.random.uniform(jax.random.fold_in(jax.random.fold_in(rng, 6), axis_at), (shards_of,), jnp.float32, low / len(shards), high / len(shards))
        return jnp.repeat(jnp.exp(heights), extent[axis_at] // shards_of).reshape((-1,) + (1,) * (len(extent) - axis_at - 1))

    loudness = one(*shards[0])
    for cut in shards[1:]:
        loudness = loudness * one(*cut)
    return loudness


def scatter_about(stream_key, dims, deviation, most, cuts=(), held_as=jnp.bfloat16):
    result = jax.random.normal(stream_key, dims, jnp.float32) * deviation
    if len(cuts) > 0:
        result = steps_of(stream_key, dims, cuts, -0.22, 0.18) * result
    return jnp.clip(result, min=-most, max=most).astype(held_as)


def setup_inputs(seed: int = 0) -> dict:
    key_of = jax.random.split(jax.random.key(seed), 8)
    feature_codes = scatter_about(key_of[0], (NODES, F), 1.0, 6.0, ((0, 64), (1, 2)))
    group_scales = jnp.clip(jnp.exp(math.log(2.0) - 2.0794415 * jax.random.uniform(key_of[1], (NODES, F // GROUP), jnp.float32) ** steps_of(key_of[1], (NODES, F // GROUP), ((0, 64), (1, 2)), -0.2, 0.2)), 0.25, 2.0)
    adjacency = draw_adjacency(jax.random.fold_in(key_of[7], 71), 0)
    tile_source = draw_tile_source(jax.random.fold_in(key_of[7], 71), 0)
    tile_target = draw_tile_target(jax.random.fold_in(key_of[7], 71), 0)
    weight = scatter_about(key_of[5], (2 * F, FO), (2 * F) ** -0.5, 0.1875)
    out_bias = scatter_about(key_of[6], (FO,), 0.5, 3.0, ((0, 2),), jnp.float32)
    return {"feature_codes": feature_codes, "group_scales": group_scales, "adjacency": adjacency, "tile_source": tile_source, "tile_target": tile_target, "weight": weight, "out_bias": out_bias}


def reference(feature_codes, group_scales, adjacency, tile_source, tile_target, weight, out_bias):
    scaled = feature_codes.astype(jnp.float32).reshape(NODES, F // GROUP, GROUP) * group_scales[:, :, None]
    features = scaled.reshape(NODES, F).astype(jnp.bfloat16)
    node_tiles = features.reshape(NODES // TILE, TILE, F)

    def per_block(block_id):
        begin = block_id * TILES_DEV
        blocks = lax.dynamic_slice_in_dim(adjacency, begin, TILES_DEV, 0).astype(jnp.float32)
        sources = lax.dynamic_slice_in_dim(tile_source, begin, TILES_DEV, 0)
        targets = lax.dynamic_slice_in_dim(tile_target, begin, TILES_DEV, 0)
        picked = jnp.take(node_tiles, sources, axis=0).astype(jnp.float32)
        products = jnp.einsum('tij,tjf->tif', blocks, picked)
        totals = jnp.zeros((NTD, TILE, F), jnp.float32).at[targets].add(products)
        degree = jnp.zeros((NTD, TILE), jnp.float32).at[targets].add(lax.optimization_barrier(jnp.sum(blocks, axis=2)))
        return (totals / jnp.sqrt(1.0 + degree)[:, :, None]).astype(jnp.bfloat16)
    neighbours = lax.map(per_block, jnp.arange(N_BLK, dtype=jnp.int32)).reshape(NODES, F)
    joined = jnp.concatenate([features, neighbours], axis=1)
    summed = jnp.dot(joined, weight, preferred_element_type=jnp.float32) + out_bias
    return jnp.maximum(summed, 0.0).astype(jnp.bfloat16)
```

```python
import functools

import jax
import jax.numpy as jnp
import numpy as np
from jax import lax
from jax.experimental import pallas as pl
from jax.experimental.pallas import tpu as pltpu
from jax.sharding import PartitionSpec as P

F = 512
TILE = 128
NTD = 4
EXTENT = (4, 2, 4, 2, 2)
SLOTS = 4


def coordinates():
    return [tuple(int(v) for v in c) for c in np.ndindex(*EXTENT)]


def linear(c):
    return int(np.ravel_multi_index(tuple(v % e for v, e in zip(c, EXTENT)), EXTENT))


class Piece:
    def __init__(self, value, tiles):
        self.value = value
        self.tiles = tiles

    def rows(self, begin, end):
        return Piece(self.value[begin * TILE : end * TILE], self.tiles[:, begin:end])


def join(*pieces):
    return Piece(
        jnp.concatenate([p.value for p in pieces], axis=0),
        np.concatenate([p.tiles for p in pieces], axis=1),
    )


def moved(piece, where):
    pairs = [(linear(c), linear(where(*c))) for c in coordinates()]
    tiles = np.empty_like(piece.tiles)
    for source, target in pairs:
        tiles[target] = piece.tiles[source]
    return Piece(lax.ppermute(piece.value, ("blk", "rep"), pairs), tiles)


def first_axis(piece, steps):
    return moved(
        piece,
        lambda y, h, x, c, z: (y, h, x + steps, c, z) if c == 0 else (y + steps, h, x, c, z),
    )


def second_axis(piece, steps):
    return moved(
        piece,
        lambda y, h, x, c, z: (y + steps, h, x, c, z) if c == 0 else (y, h, x + steps, c, z),
    )


def over_z(piece):
    return moved(piece, lambda y, h, x, c, z: (y, h + 1, x, c, z))


def other_core(piece):
    return moved(piece, lambda y, h, x, c, z: (y, h, x, 1 - c, z))


def degree_kernel(target_ref, adjacency_ref, total_ref):
    step = pl.program_id(0)
    count = adjacency_ref.shape[0]

    @pl.when(step == 0)
    def _():
        total_ref[...] = jnp.zeros_like(total_ref)

    def add(k, carry):
        at = target_ref[step * count + k]
        total_ref[at] += adjacency_ref[k].astype(jnp.float32)
        return carry

    lax.fori_loop(0, count, add, 0, unroll=4)


def degree_lanes(adjacency, tile_target):
    count = adjacency.shape[0]
    step = 64
    return pl.pallas_call(
        degree_kernel,
        grid_spec=pltpu.PrefetchScalarGridSpec(
            num_scalar_prefetch=1,
            grid=(count // step,),
            in_specs=[pl.BlockSpec((step, TILE, TILE), lambda i, t: (i, 0, 0))],
            out_specs=pl.BlockSpec((NTD, TILE, TILE), lambda i, t: (0, 0, 0)),
        ),
        out_shape=jax.ShapeDtypeStruct((NTD, TILE, TILE), jnp.float32),
        compiler_params=pltpu.CompilerParams(vmem_limit_bytes=16 * 2**20),
        cost_estimate=pl.CostEstimate(
            flops=count * TILE * TILE, bytes_accessed=count * TILE * TILE * 2, transcendentals=0
        ),
        name="degree",
    )(tile_target, adjacency)


def gather_kernel(chunks, last, ids_ref, table_ref, adjacency_ref, *refs):
    pieces = refs[: len(chunks)]
    rest = refs[len(chunks) :]
    if last:
        total_in, lanes_ref, own_ref, out_ref = rest[:4]
        rest = rest[4:]
    else:
        total_in, out_ref = rest[:2]
        rest = rest[2:]
    blank, dense, rows, total, tile_sem, row_sem = rest
    steps = [(p, s) for p, n in enumerate(chunks) for s in range(n)]
    wide = NTD * TILE
    blank[...] = jnp.zeros_like(blank)

    def begin(i):
        slot = i % SLOTS
        p, s = steps[i]

        def one(q, carry):
            j = q // NTD
            t = q % NTD
            k = table_ref[ids_ref[i * NTD + j] * NTD + t]
            place = dense.at[
                slot,
                pl.ds(pl.multiple_of(t * TILE, TILE), TILE),
                pl.ds(pl.multiple_of(j * TILE, TILE), TILE),
            ]

            @pl.when(k >= 0)
            def _():
                pltpu.make_async_copy(
                    adjacency_ref.at[jnp.maximum(k, 0)], place, tile_sem.at[slot]
                ).start()

            @pl.when(k < 0)
            def _():
                pltpu.make_async_copy(blank, place, tile_sem.at[slot]).start()

            return carry

        lax.fori_loop(0, NTD * NTD, one, 0, unroll=True)
        pltpu.make_async_copy(
            pieces[p].at[pl.ds(s * wide, wide)], rows.at[slot], row_sem.at[slot]
        ).start()

    for i in range(min(SLOTS - 1, len(steps))):
        begin(i)
    total[...] = total_in[...]
    for i in range(len(steps)):
        slot = i % SLOTS
        if i + SLOTS - 1 < len(steps):
            begin(i + SLOTS - 1)
        pltpu.make_async_copy(dense.at[slot], dense.at[slot], tile_sem.at[slot]).wait()
        pltpu.make_async_copy(rows.at[slot], rows.at[slot], row_sem.at[slot]).wait()
        total[...] += jnp.dot(dense[slot], rows[slot], preferred_element_type=jnp.float32)
    if last:
        degree = jnp.sum(lanes_ref[...], axis=1, keepdims=True)
        near = total[...] / jnp.sqrt(1.0 + degree)
        out_ref[...] = jnp.maximum(near + own_ref[...], 0.0).astype(out_ref.dtype)
    else:
        out_ref[...] = total[...]


def gathered(pieces, device, table, adjacency, total, ending=None):
    tiles = np.concatenate([p.tiles for p in pieces], axis=1)
    ids = lax.dynamic_index_in_dim(jnp.asarray(tiles, jnp.int32), device, 0, keepdims=False)
    chunks = [p.value.shape[0] // (NTD * TILE) for p in pieces]
    width = total.shape[1]
    wide = NTD * TILE
    whole = pl.BlockSpec(memory_space=pltpu.VMEM)
    scalars = pl.BlockSpec(memory_space=pltpu.SMEM)
    there = pl.BlockSpec(memory_space=pl.ANY)
    extra = [] if ending is None else list(ending)
    count = sum(chunks)
    return pl.pallas_call(
        functools.partial(gather_kernel, chunks, ending is not None),
        in_specs=[scalars, scalars, there] + [there] * len(pieces) + [whole] * (1 + len(extra)),
        out_specs=whole,
        out_shape=jax.ShapeDtypeStruct(
            (wide, width), jnp.float32 if ending is None else jnp.bfloat16
        ),
        scratch_shapes=[
            pltpu.VMEM((TILE, TILE), jnp.bfloat16),
            pltpu.VMEM((SLOTS, wide, wide), jnp.bfloat16),
            pltpu.VMEM((SLOTS, wide, width), jnp.bfloat16),
            pltpu.VMEM((wide, width), jnp.float32),
            pltpu.SemaphoreType.DMA((SLOTS,)),
            pltpu.SemaphoreType.DMA((SLOTS,)),
        ],
        compiler_params=pltpu.CompilerParams(vmem_limit_bytes=16 * 2**20),
        cost_estimate=pl.CostEstimate(
            flops=2 * count * wide * wide * width,
            bytes_accessed=count * wide * (wide + width),
            transcendentals=0,
        ),
        name="gather",
    )(ids, table, adjacency, *[p.value for p in pieces], total, *extra)


def body(feature_codes, group_scales, adjacency, tile_source, tile_target, weight, out_bias):
    rows, half = feature_codes.shape
    groups = group_scales.shape[1]
    scaled = (
        feature_codes.astype(jnp.float32).reshape(rows, groups, half // groups)
        * group_scales[:, :, None]
    )
    features = scaled.reshape(rows, half).astype(jnp.bfloat16)
    side = lax.axis_index("rep")
    device = lax.axis_index("blk") * 2 + side
    pairs = [(linear(c), linear(c[:4] + (1 - c[4],))) for c in coordinates()]
    across = lax.ppermute(features, ("blk", "rep"), pairs)

    cols = out_bias.shape[0]

    def part(begin, whose):
        return lax.dynamic_slice(weight, (begin + whose * half, side * cols), (half, cols))

    def times(x, w):
        return jnp.dot(x, w, preferred_element_type=jnp.float32)

    sent = times(features, part(F, side)) + times(across, part(F, 1 - side))
    own = times(features, part(0, side)) + times(across, part(0, 1 - side)) + out_bias
    lanes = degree_lanes(adjacency, tile_target).reshape(NTD * TILE, TILE)

    count = tile_source.shape[0]
    spots = jnp.arange(EXTENT[0] * EXTENT[1] * EXTENT[2] * EXTENT[3] * NTD * NTD, dtype=jnp.int32)
    here = tile_source * NTD + tile_target
    table = jnp.max(
        jnp.where(
            here[None, :] == spots[:, None], jnp.arange(count, dtype=jnp.int32)[None, :], -1
        ),
        axis=1,
    )

    blocks = np.array([linear(c) // 2 for c in coordinates()])
    mine = Piece(
        sent.astype(jnp.bfloat16), blocks[:, None] * NTD + np.arange(NTD)[None, :]
    )

    plus, minus, over = (first_axis(mine, s) for s in (1, -1, 2))
    z_mine = over_z(mine)
    line = join(mine, plus, minus, over)
    z_line = join(z_mine, over_z(plus), over_z(minus), over_z(over))
    total = jnp.zeros((NTD * TILE, cols), jnp.float32)
    seen = []

    def absorb(total, pieces, ending=None):
        pieces = list(pieces) + [other_core(p) for p in pieces]
        seen.extend(p.tiles for p in pieces)
        return gathered(pieces, device, table, adjacency, total, ending)

    total = absorb(total, [line])
    ends = []
    for source in (line, z_line):
        up, down = second_axis(source, 1), second_axis(source, -1)
        mid = source.tiles.shape[1] // 2
        ends.append((up, down, second_axis(up.rows(0, mid), 1), second_axis(down.rows(mid, 2 * mid), -1)))
    total = absorb(total, ends[0][:2])
    total = absorb(total, [z_line])
    total = absorb(total, ends[0][2:])
    total = absorb(total, ends[1][:2])
    result = absorb(total, ends[1][2:], (lanes, own))
    every = np.sort(np.concatenate(seen, axis=1), axis=1)
    assert (every == np.arange(every.shape[1])[None, :]).all() and every.shape[1] == spots.size // NTD
    return result


def solution(mesh):
    placed = (
        P("blk", "rep"),
        P("blk", "rep"),
        P("blk", None, None),
        P("blk"),
        P("blk"),
        P(),
        P("rep"),
    )
    return jax.shard_map(
        body, mesh=mesh, in_specs=placed, out_specs=P("blk", "rep"), check_vma=False
    )
```

```python
import functools

import jax
import jax.numpy as jnp
import numpy as np
from jax import lax
from jax.experimental import pallas as pl
from jax.experimental.pallas import tpu as pltpu
from jax.sharding import PartitionSpec as P

F = 512
TILE = 128
NTD = 4
EXTENT = (4, 2, 4, 2, 2)
VMEM_LIMIT = 8 * 2**20
TOGETHER = 4
HINT = 40


def coordinates():
    return [tuple(int(v) for v in c) for c in np.ndindex(*EXTENT)]


def linear(c):
    return int(np.ravel_multi_index(tuple(v % e for v, e in zip(c, EXTENT)), EXTENT))


class Piece:
    def __init__(self, value, tiles):
        self.value = value
        self.tiles = tiles

    def rows(self, begin, end):
        value = None if self.value is None else self.value[begin * TILE : end * TILE]
        return Piece(value, self.tiles[:, begin:end])

    def halves(self):
        count = self.tiles.shape[1]
        return self.rows(0, count // 2), self.rows(count // 2, count)


def join(*pieces):
    planned = pieces[0].value is None
    return Piece(
        None if planned else jnp.concatenate([p.value for p in pieces], axis=0),
        np.concatenate([p.tiles for p in pieces], axis=1),
    )


def moved(piece, where):
    pairs = [(linear(c), linear(where(*c))) for c in coordinates()]
    tiles = np.empty_like(piece.tiles)
    for source, target in pairs:
        tiles[target] = piece.tiles[source]
    value = piece.value
    if value is not None:
        value = lax.ppermute(value, ("blk", "rep"), pairs)
    return Piece(value, tiles)


def first_axis(piece, steps):
    return moved(
        piece,
        lambda y, h, x, c, z: (y, h, x + steps, c, z) if c == 0 else (y + steps, h, x, c, z),
    )


def second_axis(piece, steps):
    return moved(
        piece,
        lambda y, h, x, c, z: (y + steps, h, x, c, z) if c == 0 else (y, h, x + steps, c, z),
    )


def over_z(piece):
    return moved(piece, lambda y, h, x, c, z: (y, h + 1, x, c, z))


def other_core(piece):
    return moved(piece, lambda y, h, x, c, z: (y, h, x, 1 - c, z))


def after(piece, others):
    if piece.value is None:
        return piece
    return Piece(lax.optimization_barrier((piece.value, *others))[0], piece.tiles)


def plan(mine, absorb):
    plus, minus, over = (first_axis(mine, s) for s in (1, -1, 2))
    z_mine = over_z(mine)
    z_pair = over_z(join(plus, minus))
    near = join(mine, plus, minus, over, z_mine)
    near_up, near_down = second_axis(near, 1), second_axis(near, -1)
    z_over = first_axis(z_mine, 2)
    absorb([near, other_core(near)])
    far = join(z_pair, z_over)
    far_up = second_axis(join(far, near_up.rows(0, 3 * NTD)), 1)
    far_down = second_axis(join(far, near_down.rows(3 * NTD, 5 * NTD)), -1)
    absorb([near_up, near_down, other_core(near_up), other_core(near_down)])
    done = absorb([far, other_core(far)])
    end = join(
        second_axis(after(far_up.rows(0, NTD), (done,)), 1),
        second_axis(after(far_down.rows(NTD, 3 * NTD), (done,)), -1),
    )
    absorb([far_up, far_down])
    absorb([other_core(far_up), other_core(far_down)])
    absorb([end, other_core(end)], True)


def start_kernel(side_ref, codes_hbm, scales_hbm, weight_hbm, features_ref, weights_ref, codes_ref, scales_ref, sems):
    rows, half = codes_ref.shape
    groups = scales_ref.shape[0]
    width = half // groups
    cols = weights_ref.shape[2]
    side = side_ref[0]
    inputs = [
        pltpu.make_async_copy(codes_hbm, codes_ref, sems.at[0]),
        pltpu.make_async_copy(scales_hbm, scales_ref, sems.at[1]),
    ]
    for n in range(4):
        whose = side if n % 2 == 0 else 1 - side
        at = pl.ds(pl.multiple_of((n // 2) * F + whose * half, half), half)
        from_here = weight_hbm.at[at, pl.ds(pl.multiple_of(side * cols, cols), cols)]
        inputs.append(pltpu.make_async_copy(from_here, weights_ref.at[n], sems.at[2 + n]))
    for copy in inputs:
        copy.start()
    for copy in inputs[:2]:
        copy.wait()
    for g in range(groups):
        at = slice(g * width, (g + 1) * width)
        scales = jnp.broadcast_to(scales_ref[g : g + 1, :], (width, rows)).T
        scaled = codes_ref[:, at].astype(jnp.float32) * scales
        features_ref[:, at] = scaled.astype(features_ref.dtype)
    for copy in inputs[2:]:
        copy.wait()


def start(side, codes, scales, weight, cols):
    rows, half = codes.shape
    there = pl.BlockSpec(memory_space=pl.ANY)
    whole = pl.BlockSpec(memory_space=pltpu.VMEM)
    scales = scales.T
    far = [pltpu.with_memory_space_constraint(x, pltpu.HBM) for x in (codes, scales, weight)]
    return pl.pallas_call(
        start_kernel,
        in_specs=[pl.BlockSpec(memory_space=pltpu.SMEM)] + [there] * 3,
        out_specs=[whole, whole],
        out_shape=[pltpu.VMEM((rows, half), codes.dtype), pltpu.VMEM((4, half, cols), weight.dtype)],
        scratch_shapes=[
            pltpu.VMEM((rows, half), codes.dtype),
            pltpu.VMEM(scales.shape, scales.dtype),
            pltpu.SemaphoreType.DMA((6,)),
        ],
        compiler_params=pltpu.CompilerParams(vmem_limit_bytes=VMEM_LIMIT),
        name="start",
    )(side[None], *far)


def mix_kernel(first, features_ref, across_ref, weights_ref, *refs):
    out_ref = refs[-1]
    mixed = jnp.dot(features_ref[...], weights_ref[first], preferred_element_type=jnp.float32)
    mixed += jnp.dot(across_ref[...], weights_ref[first + 1], preferred_element_type=jnp.float32)
    for bias_ref in refs[:-1]:
        mixed += bias_ref[...]
    out_ref[...] = mixed.astype(out_ref.dtype)


def mix(first, features, across, weights, dtype, *bias):
    whole = pl.BlockSpec(memory_space=pltpu.VMEM)
    return pl.pallas_call(
        functools.partial(mix_kernel, first),
        in_specs=[whole] * (3 + len(bias)),
        out_specs=whole,
        out_shape=pltpu.VMEM((features.shape[0], weights.shape[2]), dtype),
        compiler_params=pltpu.CompilerParams(vmem_limit_bytes=VMEM_LIMIT),
        name="mix",
    )(features, across, weights, *bias)


def load_kernel(
    parts,
    device_ref,
    spots_hbm,
    source_hbm,
    target_hbm,
    adjacency_hbm,
    tiles_ref,
    lanes_ref,
    table_ref,
    spots_ref,
    source_ref,
    target_ref,
    sems,
):
    count = adjacency_hbm.shape[0]
    step = count // parts

    def copy(i):
        at = pl.ds(i * step, step)
        return pltpu.make_async_copy(adjacency_hbm.at[at], tiles_ref.at[at], sems.at[i])

    scalars = [
        pltpu.make_async_copy(spots_hbm.at[device_ref[0]], spots_ref, sems.at[parts]),
        pltpu.make_async_copy(source_hbm, source_ref, sems.at[parts + 1]),
        pltpu.make_async_copy(target_hbm, target_ref, sems.at[parts + 2]),
    ]
    for c in scalars:
        c.start()
    for i in range(parts):
        copy(i).start()
    tiles_ref[count] = jnp.zeros_like(tiles_ref[count])
    lanes_ref[...] = jnp.zeros_like(lanes_ref)

    def blank(k, carry):
        table_ref[k] = count
        return carry

    lax.fori_loop(0, table_ref.shape[0], blank, 0, unroll=16)
    for c in scalars:
        c.wait()

    def add(k, carry):
        target = target_ref[k]
        source = source_ref[k]
        table_ref[spots_ref[source // TILE, source % TILE] * NTD + target] = k
        lanes_ref[target] += tiles_ref[k].astype(jnp.float32)
        return carry

    for i in range(parts):
        copy(i).wait()
        lax.fori_loop(i * step, (i + 1) * step, add, 0, unroll=4)


def load(device, spots, adjacency, tile_source, tile_target):
    count = adjacency.shape[0]
    parts = 16
    there = pl.BlockSpec(memory_space=pl.ANY)
    whole = pl.BlockSpec(memory_space=pltpu.VMEM)
    scalars = pl.BlockSpec(memory_space=pltpu.SMEM)
    nodes = spots.shape[1]
    spots = jnp.asarray(spots.reshape(-1, nodes // TILE, TILE), jnp.int32)
    far = [
        pltpu.with_memory_space_constraint(x, pltpu.HBM)
        for x in (spots, tile_source, tile_target, adjacency)
    ]
    return pl.pallas_call(
        functools.partial(load_kernel, parts),
        in_specs=[scalars] + [there] * 4,
        out_specs=[whole, whole, scalars],
        out_shape=[
            pltpu.VMEM((count + 1, TILE, TILE), adjacency.dtype),
            pltpu.VMEM((NTD, TILE, TILE), jnp.float32),
            jax.ShapeDtypeStruct((nodes * NTD,), jnp.int32),
        ],
        scratch_shapes=[
            pltpu.SMEM((nodes // TILE, TILE), jnp.int32),
            pltpu.SMEM((count,), jnp.int32),
            pltpu.SMEM((count,), jnp.int32),
            pltpu.SemaphoreType.DMA((parts + 3,)),
        ],
        compiler_params=pltpu.CompilerParams(vmem_limit_bytes=VMEM_LIMIT),
        cost_estimate=pl.CostEstimate(
            flops=count * TILE * TILE, bytes_accessed=count * TILE * TILE * 2, transcendentals=0
        ),
        name="load",
    )(device[None], *far)


def gather_kernel(chunks, offset, first, last, table_ref, tiles_ref, *refs):
    pieces = refs[: len(chunks)]
    rest = refs[len(chunks) :]
    if last:
        total_in, lanes_ref, own_ref, out_ref, total = rest
        total[...] = total_in[...]
    elif first:
        (total,) = rest
        total[...] = jnp.zeros_like(total)
    else:
        total_in, total = rest
        total[...] = total_in[...]
    wide = NTD * TILE

    def product(piece, s, blocks, base):
        at = (base + s * NTD) * NTD

        def tile(t, j):
            return tiles_ref[table_ref[at + j * NTD + t]]

        left = jnp.concatenate(
            [
                jnp.concatenate([tile(t, j) for j in range(blocks * NTD)], axis=1)
                for t in range(NTD)
            ],
            axis=0,
        )
        right = piece[pl.ds(pl.multiple_of(s * wide, wide), blocks * wide)]
        return jnp.dot(left, right, preferred_element_type=jnp.float32)

    base = offset
    for piece, count in zip(pieces, chunks):

        def step(i, carry, piece=piece, base=base):
            total[...] += product(piece, i * TOGETHER, TOGETHER, base)
            return carry

        lax.fori_loop(0, count // TOGETHER, step, 0)
        if count % TOGETHER:
            total[...] += product(piece, count - count % TOGETHER, count % TOGETHER, base)
        base += count * NTD
    if last:
        degree = jnp.sum(lanes_ref[...], axis=1, keepdims=True)
        near = total[...] / jnp.sqrt(1.0 + degree)
        out_ref[...] = jnp.maximum(near + own_ref[...], 0.0).astype(out_ref.dtype)


def gathered(pieces, offset, table, tiles, width, total=None, ending=None):
    tiles = pltpu.with_memory_space_constraint(tiles, pltpu.VMEM)
    chunks = [p.value.shape[0] // (NTD * TILE) for p in pieces]
    wide = NTD * TILE
    whole = pl.BlockSpec(memory_space=pltpu.VMEM)
    scalars = pl.BlockSpec(memory_space=pltpu.SMEM)
    extra = ([] if total is None else [total]) + ([] if ending is None else list(ending))
    count = sum(chunks)
    last = ending is not None
    return pl.pallas_call(
        functools.partial(gather_kernel, chunks, offset, total is None, last),
        in_specs=[scalars, whole] + [whole] * (len(pieces) + len(extra)),
        out_specs=whole,
        out_shape=jax.ShapeDtypeStruct((wide, width), jnp.bfloat16 if last else jnp.float32),
        scratch_shapes=[pltpu.VMEM((wide, width), jnp.float32)] if last else [],
        compiler_params=pltpu.CompilerParams(vmem_limit_bytes=VMEM_LIMIT),
        cost_estimate=pl.CostEstimate(
            flops=HINT * count * wide * wide * width,
            bytes_accessed=count * wide * (wide + width),
            transcendentals=0,
        ),
        name="gather",
    )(table, tiles, *[p.value for p in pieces], *extra)


def body(feature_codes, group_scales, adjacency, tile_source, tile_target, weight, out_bias):
    cols = out_bias.shape[0]
    side = lax.axis_index("rep")
    device = lax.axis_index("blk") * 2 + side
    features, weights = start(side, feature_codes, group_scales, weight, cols)
    blocks = np.array([linear(c) // 2 for c in coordinates()])
    here = Piece(features, blocks[:, None] * NTD + np.arange(NTD)[None, :])
    across = moved(here, lambda y, h, x, c, z: (y, h, x, c, 1 - z))
    taken = []
    plan(Piece(None, here.tiles), lambda pieces, ending=False: taken.extend(p.tiles for p in pieces))
    order = np.concatenate(taken, axis=1)
    spots = np.argsort(order, axis=1)
    every = np.arange(lax.axis_size("blk") * NTD)
    assert np.array_equal(np.sort(order, axis=1), np.broadcast_to(every, order.shape))
    tiles, lanes, table = load(device, spots, adjacency, tile_source, tile_target)
    near, lanes = lax.optimization_barrier((across.value, lanes))
    lanes = lanes.reshape(NTD * TILE, TILE)
    sent = mix(2, features, near, weights, jnp.bfloat16)
    own = mix(0, features, near, weights, jnp.float32, out_bias[None])

    total = [None]
    place = [0]

    def absorb(pieces, ending=False):
        total[0] = gathered(
            pieces, place[0], table, tiles, cols, total[0], (lanes, own) if ending else None
        )
        place[0] += sum(p.tiles.shape[1] for p in pieces)
        return total[0]

    plan(Piece(sent, here.tiles), absorb)
    return total[0]


def solution(mesh):
    placed = (
        P("blk", "rep"),
        P("blk", "rep"),
        P("blk", None, None),
        P("blk"),
        P("blk"),
        P(),
        P("rep"),
    )
    return jax.shard_map(
        body, mesh=mesh, in_specs=placed, out_specs=P("blk", "rep"), check_vma=False
    )
```

```python
import functools

import jax
import jax.numpy as jnp
import numpy as np
from jax import lax
from jax.experimental import pallas as pl
from jax.experimental.pallas import tpu as pltpu
from jax.sharding import PartitionSpec as P

F = 512
TILE = 128
NTD = 4
EXTENT = (4, 2, 4, 2, 2)
VMEM_LIMIT = 8 * 2**20
TOGETHER = 16
HINT = 40


def coordinates():
    return [tuple(int(v) for v in c) for c in np.ndindex(*EXTENT)]


def linear(c):
    return int(np.ravel_multi_index(tuple(v % e for v, e in zip(c, EXTENT)), EXTENT))


class Piece:
    def __init__(self, value, tiles):
        self.value = value
        self.tiles = tiles

    def rows(self, begin, end):
        value = None if self.value is None else self.value[begin * TILE : end * TILE]
        return Piece(value, self.tiles[:, begin:end])

    def halves(self):
        count = self.tiles.shape[1]
        return self.rows(0, count // 2), self.rows(count // 2, count)


def join(*pieces):
    planned = pieces[0].value is None
    return Piece(
        None if planned else jnp.concatenate([p.value for p in pieces], axis=0),
        np.concatenate([p.tiles for p in pieces], axis=1),
    )


def moved(piece, where):
    pairs = [(linear(c), linear(where(*c))) for c in coordinates()]
    tiles = np.empty_like(piece.tiles)
    for source, target in pairs:
        tiles[target] = piece.tiles[source]
    value = piece.value
    if value is not None:
        value = lax.ppermute(value, ("blk", "rep"), pairs)
    return Piece(value, tiles)


def first_axis(piece, steps):
    return moved(
        piece,
        lambda y, h, x, c, z: (y, h, x + steps, c, z) if c == 0 else (y + steps, h, x, c, z),
    )


def second_axis(piece, steps):
    return moved(
        piece,
        lambda y, h, x, c, z: (y + steps, h, x, c, z) if c == 0 else (y, h, x + steps, c, z),
    )


def over_z(piece):
    return moved(piece, lambda y, h, x, c, z: (y, h + 1, x, c, z))


def other_core(piece):
    return moved(piece, lambda y, h, x, c, z: (y, h, x, 1 - c, z))


def after(piece, others):
    if piece.value is None:
        return piece
    return Piece(lax.optimization_barrier((piece.value, *others))[0], piece.tiles)


def plan(mine, absorb):
    plus, minus, over = (first_axis(mine, s) for s in (1, -1, 2))
    z_mine = over_z(mine)
    z_pair = over_z(join(plus, minus))
    near = join(mine, plus, minus, over, z_mine)
    near_up, near_down = second_axis(near, 1), second_axis(near, -1)
    z_over = first_axis(z_mine, 2)
    far = join(z_pair, z_over)
    rest = far.rows(NTD, 3 * NTD)
    far_up = second_axis(join(rest, near_up.halves()[0]), 1)
    far_down = second_axis(join(rest, near_down.halves()[1]), -1)
    z_sides = over_z(join(near_up.rows(NTD, 2 * NTD), near_down.rows(NTD, 2 * NTD)))
    absorb([near, other_core(near)])
    done = absorb([near_up, near_down, other_core(near_up), other_core(near_down)])
    absorb([far, other_core(far)])
    half = NTD // 2
    end_up = join(far_up.rows(0, NTD), z_sides.rows(0, half))
    end_down = join(far_down.rows(NTD, 2 * NTD), z_sides.rows(NTD + half, 2 * NTD))
    end = join(second_axis(end_up, 1), second_axis(end_down, -1))
    absorb([far_up, far_down, z_sides])
    absorb([other_core(far_up), other_core(far_down), other_core(after(z_sides, (done,)))])
    absorb([end, other_core(end)], ending=True)


def start_kernel(side_ref, codes_hbm, scales_hbm, weight_hbm, features_ref, weights_ref, codes_ref, scales_ref, sems):
    rows, half = codes_ref.shape
    groups = scales_ref.shape[0]
    width = half // groups
    cols = weights_ref.shape[2]
    side = side_ref[0]
    inputs = [
        pltpu.make_async_copy(codes_hbm, codes_ref, sems.at[0]),
        pltpu.make_async_copy(scales_hbm, scales_ref, sems.at[1]),
    ]
    for n in range(4):
        whose = side if n % 2 == 0 else 1 - side
        at = pl.ds(pl.multiple_of((n // 2) * F + whose * half, half), half)
        from_here = weight_hbm.at[at, pl.ds(pl.multiple_of(side * cols, cols), cols)]
        inputs.append(pltpu.make_async_copy(from_here, weights_ref.at[n], sems.at[2 + n]))
    for copy in inputs:
        copy.start()
    for copy in inputs[:2]:
        copy.wait()
    for g in range(groups):
        at = slice(g * width, (g + 1) * width)
        scales = jnp.broadcast_to(scales_ref[g : g + 1, :], (width, rows)).T
        scaled = codes_ref[:, at].astype(jnp.float32) * scales
        features_ref[:, at] = scaled.astype(features_ref.dtype)
    for copy in inputs[2:]:
        copy.wait()


def start(side, codes, scales, weight, cols):
    rows, half = codes.shape
    there = pl.BlockSpec(memory_space=pl.ANY)
    whole = pl.BlockSpec(memory_space=pltpu.VMEM)
    scales = scales.T
    far = [pltpu.with_memory_space_constraint(x, pltpu.HBM) for x in (codes, scales, weight)]
    return pl.pallas_call(
        start_kernel,
        in_specs=[pl.BlockSpec(memory_space=pltpu.SMEM)] + [there] * 3,
        out_specs=[whole, whole],
        out_shape=[pltpu.VMEM((rows, half), codes.dtype), pltpu.VMEM((4, half, cols), weight.dtype)],
        scratch_shapes=[
            pltpu.VMEM((rows, half), codes.dtype),
            pltpu.VMEM(scales.shape, scales.dtype),
            pltpu.SemaphoreType.DMA((6,)),
        ],
        compiler_params=pltpu.CompilerParams(vmem_limit_bytes=VMEM_LIMIT),
        name="start",
    )(side[None], *far)


def mix_kernel(first, features_ref, across_ref, weights_ref, *refs):
    out_ref = refs[-1]
    mixed = jnp.dot(features_ref[...], weights_ref[first], preferred_element_type=jnp.float32)
    mixed += jnp.dot(across_ref[...], weights_ref[first + 1], preferred_element_type=jnp.float32)
    for bias_ref in refs[:-1]:
        mixed += bias_ref[...]
    out_ref[...] = mixed.astype(out_ref.dtype)


def mix(first, features, across, weights, dtype, *bias):
    whole = pl.BlockSpec(memory_space=pltpu.VMEM)
    return pl.pallas_call(
        functools.partial(mix_kernel, first),
        in_specs=[whole] * (3 + len(bias)),
        out_specs=whole,
        out_shape=pltpu.VMEM((features.shape[0], weights.shape[2]), dtype),
        compiler_params=pltpu.CompilerParams(vmem_limit_bytes=VMEM_LIMIT),
        name="mix",
    )(features, across, weights, *bias)


def load_kernel(
    parts,
    device_ref,
    spots_hbm,
    source_hbm,
    target_hbm,
    adjacency_hbm,
    tiles_ref,
    table_ref,
    spots_ref,
    source_ref,
    target_ref,
    sems,
):
    count = adjacency_hbm.shape[0]
    step = count // parts

    def copy(i):
        at = pl.ds(i * step, step)
        return pltpu.make_async_copy(adjacency_hbm.at[at], tiles_ref.at[at], sems.at[i])

    scalars = [
        pltpu.make_async_copy(spots_hbm.at[device_ref[0]], spots_ref, sems.at[parts]),
        pltpu.make_async_copy(source_hbm, source_ref, sems.at[parts + 1]),
        pltpu.make_async_copy(target_hbm, target_ref, sems.at[parts + 2]),
    ]
    for c in scalars:
        c.start()
    for i in range(parts):
        copy(i).start()
    tiles_ref[count] = jnp.zeros_like(tiles_ref[count])
    def blank(k, carry):
        table_ref[k] = count
        return carry

    lax.fori_loop(0, table_ref.shape[0], blank, 0, unroll=16)
    for c in scalars:
        c.wait()

    def add(k, carry):
        target = target_ref[k]
        source = source_ref[k]
        table_ref[spots_ref[source // TILE, source % TILE] * NTD + target] = k
        return carry

    lax.fori_loop(0, count, add, 0, unroll=8)
    for i in range(parts):
        copy(i).wait()


def degree_kernel(target_ref, tiles_ref, lanes_ref, even, odd):
    even[...] = jnp.zeros_like(even)
    odd[...] = jnp.zeros_like(odd)

    def add(k, carry):
        even[target_ref[2 * k]] += tiles_ref[2 * k].astype(jnp.float32)
        odd[target_ref[2 * k + 1]] += tiles_ref[2 * k + 1].astype(jnp.float32)
        return carry

    lax.fori_loop(0, target_ref.shape[0] // 2, add, 0, unroll=4)
    lanes_ref[...] = even[...] + odd[...]


def degree(tiles, tile_target):
    whole = pl.BlockSpec(memory_space=pltpu.VMEM)
    count = tile_target.shape[0]
    return pl.pallas_call(
        degree_kernel,
        in_specs=[pl.BlockSpec(memory_space=pltpu.SMEM), whole],
        out_specs=whole,
        out_shape=pltpu.VMEM((NTD, TILE, TILE), jnp.float32),
        scratch_shapes=[pltpu.VMEM((NTD, TILE, TILE), jnp.float32)] * 2,
        compiler_params=pltpu.CompilerParams(vmem_limit_bytes=VMEM_LIMIT),
        cost_estimate=pl.CostEstimate(
            flops=count * TILE * TILE, bytes_accessed=count * TILE * TILE * 2, transcendentals=0
        ),
        name="degree",
    )(tile_target, pltpu.with_memory_space_constraint(tiles, pltpu.VMEM))


def load(device, spots, adjacency, tile_source, tile_target):
    count = adjacency.shape[0]
    parts = 16
    there = pl.BlockSpec(memory_space=pl.ANY)
    whole = pl.BlockSpec(memory_space=pltpu.VMEM)
    scalars = pl.BlockSpec(memory_space=pltpu.SMEM)
    nodes = spots.shape[1]
    spots = jnp.asarray(spots.reshape(-1, nodes // TILE, TILE), jnp.int32)
    far = [
        pltpu.with_memory_space_constraint(x, pltpu.HBM)
        for x in (spots, tile_source, tile_target, adjacency)
    ]
    return pl.pallas_call(
        functools.partial(load_kernel, parts),
        in_specs=[scalars] + [there] * 4,
        out_specs=[whole, scalars],
        out_shape=[
            pltpu.VMEM((count + 1, TILE, TILE), adjacency.dtype),
            jax.ShapeDtypeStruct((nodes * NTD,), jnp.int32),
        ],
        scratch_shapes=[
            pltpu.SMEM((nodes // TILE, TILE), jnp.int32),
            pltpu.SMEM((count,), jnp.int32),
            pltpu.SMEM((count,), jnp.int32),
            pltpu.SemaphoreType.DMA((parts + 3,)),
        ],
        compiler_params=pltpu.CompilerParams(vmem_limit_bytes=VMEM_LIMIT),
        cost_estimate=pl.CostEstimate(
            flops=count * TILE * TILE, bytes_accessed=count * TILE * TILE * 2, transcendentals=0
        ),
        name="load",
    )(device[None], *far)


def gather_kernel(chunks, offset, first, last, table_ref, tiles_ref, *refs):
    pieces = refs[: len(chunks)]
    rest = refs[len(chunks) :]
    if last:
        total_in, lanes_ref, own_ref, out_ref, total = rest
        total[...] = total_in[...]
    elif first:
        (total,) = rest
        total[...] = jnp.zeros_like(total)
    else:
        total_in, total = rest
        total[...] = total_in[...]
    def product(piece, s, count, base):
        at = (base + s) * NTD

        def tile(t, j):
            return tiles_ref[table_ref[at + j * NTD + t]]

        left = jnp.concatenate(
            [jnp.concatenate([tile(t, j) for j in range(count)], axis=1) for t in range(NTD)],
            axis=0,
        )
        right = piece[pl.ds(pl.multiple_of(s * TILE, TILE), count * TILE)]
        return jnp.dot(left, right, preferred_element_type=jnp.float32)

    base = offset
    for piece, count in zip(pieces, chunks):

        def step(i, carry, piece=piece, base=base):
            total[...] += product(piece, i * TOGETHER, TOGETHER, base)
            return carry

        lax.fori_loop(0, count // TOGETHER, step, 0)
        if count % TOGETHER:
            total[...] += product(piece, count - count % TOGETHER, count % TOGETHER, base)
        base += count
    if last:
        degree = jnp.sum(lanes_ref[...], axis=1, keepdims=True)
        near = total[...] / jnp.sqrt(1.0 + degree)
        out_ref[...] = jnp.maximum(near + own_ref[...], 0.0).astype(out_ref.dtype)


def gathered(pieces, offset, table, tiles, width, hint, total=None, ending=None):
    tiles = pltpu.with_memory_space_constraint(tiles, pltpu.VMEM)
    chunks = [p.value.shape[0] // TILE for p in pieces]
    wide = NTD * TILE
    whole = pl.BlockSpec(memory_space=pltpu.VMEM)
    scalars = pl.BlockSpec(memory_space=pltpu.SMEM)
    extra = ([] if total is None else [total]) + ([] if ending is None else list(ending))
    count = sum(chunks)
    last = ending is not None
    return pl.pallas_call(
        functools.partial(gather_kernel, chunks, offset, total is None, last),
        in_specs=[scalars, whole] + [whole] * (len(pieces) + len(extra)),
        out_specs=whole,
        out_shape=jax.ShapeDtypeStruct((wide, width), jnp.bfloat16 if last else jnp.float32),
        scratch_shapes=[pltpu.VMEM((wide, width), jnp.float32)] if last else [],
        compiler_params=pltpu.CompilerParams(vmem_limit_bytes=VMEM_LIMIT),
        cost_estimate=pl.CostEstimate(
            flops=hint * count * TILE * wide * width,
            bytes_accessed=count * TILE * (wide + width),
            transcendentals=0,
        ),
        name="gather",
    )(table, tiles, *[p.value for p in pieces], *extra)


def body(feature_codes, group_scales, adjacency, tile_source, tile_target, weight, out_bias):
    cols = out_bias.shape[0]
    side = lax.axis_index("rep")
    device = lax.axis_index("blk") * 2 + side
    features, weights = start(side, feature_codes, group_scales, weight, cols)
    blocks = np.array([linear(c) // 2 for c in coordinates()])
    here = Piece(features, blocks[:, None] * NTD + np.arange(NTD)[None, :])
    across = moved(here, lambda y, h, x, c, z: (y, h, x, c, 1 - z))
    taken = []
    plan(Piece(None, here.tiles), lambda pieces, *_, **__: taken.extend(p.tiles for p in pieces))
    order = np.concatenate(taken, axis=1)
    spots = np.argsort(order, axis=1)
    every = np.arange(lax.axis_size("blk") * NTD)
    assert np.array_equal(np.sort(order, axis=1), np.broadcast_to(every, order.shape))
    tiles, table = load(device, spots, adjacency, tile_source, tile_target)
    near, table = lax.optimization_barrier((across.value, table))
    table, lanes = lax.optimization_barrier((table, degree(tiles, tile_target)))
    lanes = lanes.reshape(NTD * TILE, TILE)
    sent = mix(2, features, near, weights, jnp.bfloat16)
    own = mix(0, features, near, weights, jnp.float32, out_bias[None])

    total = [None]
    place = [0]

    def absorb(pieces, hint=HINT, ending=False):
        total[0] = gathered(
            pieces, place[0], table, tiles, cols, hint, total[0], (lanes, own) if ending else None
        )
        place[0] += sum(p.tiles.shape[1] for p in pieces)
        return total[0]

    plan(Piece(sent, here.tiles), absorb)
    return total[0]


def solution(mesh):
    placed = (
        P("blk", "rep"),
        P("blk", "rep"),
        P("blk", None, None),
        P("blk"),
        P("blk"),
        P(),
        P("rep"),
    )
    return jax.shard_map(
        body, mesh=mesh, in_specs=placed, out_specs=P("blk", "rep"), check_vma=False
    )
```

```python
import functools

import jax
import jax.numpy as jnp
import numpy as np
from jax import lax
from jax.experimental import pallas as pl
from jax.experimental.pallas import tpu as pltpu
from jax.sharding import PartitionSpec as P

F = 512
TILE = 128
NTD = 4
EXTENT = (4, 2, 4, 2, 2)
VMEM_LIMIT = 8 * 2**20
TOGETHER = 16
HINT = 40


def coordinates():
    return [tuple(int(v) for v in c) for c in np.ndindex(*EXTENT)]


def linear(c):
    return int(np.ravel_multi_index(tuple(v % e for v, e in zip(c, EXTENT)), EXTENT))


class Piece:
    def __init__(self, value, tiles):
        self.value = value
        self.tiles = tiles

    def rows(self, begin, end):
        value = None if self.value is None else self.value[begin * TILE : end * TILE]
        return Piece(value, self.tiles[:, begin:end])

    def halves(self):
        count = self.tiles.shape[1]
        return self.rows(0, count // 2), self.rows(count // 2, count)


def join(*pieces):
    planned = pieces[0].value is None
    return Piece(
        None if planned else jnp.concatenate([p.value for p in pieces], axis=0),
        np.concatenate([p.tiles for p in pieces], axis=1),
    )


def moved(piece, where):
    pairs = [(linear(c), linear(where(*c))) for c in coordinates()]
    tiles = np.empty_like(piece.tiles)
    for source, target in pairs:
        tiles[target] = piece.tiles[source]
    value = piece.value
    if value is not None:
        value = lax.ppermute(value, ("blk", "rep"), pairs)
    return Piece(value, tiles)


def first_axis(piece, steps):
    return moved(
        piece,
        lambda y, h, x, c, z: (y, h, x + steps, c, z) if c == 0 else (y + steps, h, x, c, z),
    )


def second_axis(piece, steps):
    return moved(
        piece,
        lambda y, h, x, c, z: (y + steps, h, x, c, z) if c == 0 else (y, h, x + steps, c, z),
    )


def over_z(piece):
    return moved(piece, lambda y, h, x, c, z: (y, h + 1, x, c, z))


def other_core(piece):
    return moved(piece, lambda y, h, x, c, z: (y, h, x, 1 - c, z))


def after(piece, others):
    if piece.value is None:
        return piece
    return Piece(lax.optimization_barrier((piece.value, *others))[0], piece.tiles)


def plan(mine, absorb):
    plus, minus, over = (first_axis(mine, s) for s in (1, -1, 2))
    z_mine = over_z(mine)
    z_pair = over_z(join(plus, minus))
    near = join(mine, plus, minus, over, z_mine)
    near_up, near_down = second_axis(near, 1), second_axis(near, -1)
    far_up = second_axis(join(z_pair, near_up.halves()[0]), 1)
    far_down = second_axis(join(z_pair, near_down.halves()[1]), -1)
    half = NTD // 2
    at = 3 * NTD
    z_over = over_z(
        after(
            join(over, near_up.rows(at, at + half), near_down.rows(at + half, at + NTD)),
            (z_pair.value,),
        )
    )
    absorb([near, other_core(near)])
    done = absorb([near_up, near_down, other_core(near_up), other_core(near_down)])
    absorb([z_pair, other_core(z_pair)])
    end_up = join(far_up.rows(0, NTD), z_over.rows(NTD, NTD + half), z_over.rows(half, NTD))
    end_down = join(far_down.rows(NTD, 2 * NTD), z_over.rows(NTD + half, 2 * NTD), z_over.rows(0, half))
    end = join(second_axis(end_up, 1), second_axis(end_down, -1))
    absorb([far_up, far_down, z_over])
    absorb([other_core(far_up), other_core(far_down), other_core(after(z_over, (done,)))])
    absorb([end, other_core(end)], ending=True)


def start_kernel(side_ref, codes_hbm, scales_hbm, weight_hbm, features_ref, weights_ref, codes_ref, scales_ref, sems):
    rows, half = codes_ref.shape
    groups = scales_ref.shape[0]
    width = half // groups
    cols = weights_ref.shape[2]
    side = side_ref[0]
    inputs = [
        pltpu.make_async_copy(codes_hbm, codes_ref, sems.at[0]),
        pltpu.make_async_copy(scales_hbm, scales_ref, sems.at[1]),
    ]
    for n in range(4):
        whose = side if n % 2 == 0 else 1 - side
        at = pl.ds(pl.multiple_of((n // 2) * F + whose * half, half), half)
        from_here = weight_hbm.at[at, pl.ds(pl.multiple_of(side * cols, cols), cols)]
        inputs.append(pltpu.make_async_copy(from_here, weights_ref.at[n], sems.at[2 + n]))
    for copy in inputs:
        copy.start()
    for copy in inputs[:2]:
        copy.wait()
    for g in range(groups):
        at = slice(g * width, (g + 1) * width)
        scales = jnp.broadcast_to(scales_ref[g : g + 1, :], (width, rows)).T
        scaled = codes_ref[:, at].astype(jnp.float32) * scales
        features_ref[:, at] = scaled.astype(features_ref.dtype)
    for copy in inputs[2:]:
        copy.wait()


def start(side, codes, scales, weight, cols):
    rows, half = codes.shape
    there = pl.BlockSpec(memory_space=pl.ANY)
    whole = pl.BlockSpec(memory_space=pltpu.VMEM)
    scales = scales.T
    far = [pltpu.with_memory_space_constraint(x, pltpu.HBM) for x in (codes, scales, weight)]
    return pl.pallas_call(
        start_kernel,
        in_specs=[pl.BlockSpec(memory_space=pltpu.SMEM)] + [there] * 3,
        out_specs=[whole, whole],
        out_shape=[pltpu.VMEM((rows, half), codes.dtype), pltpu.VMEM((4, half, cols), weight.dtype)],
        scratch_shapes=[
            pltpu.VMEM((rows, half), codes.dtype),
            pltpu.VMEM(scales.shape, scales.dtype),
            pltpu.SemaphoreType.DMA((6,)),
        ],
        compiler_params=pltpu.CompilerParams(vmem_limit_bytes=VMEM_LIMIT),
        name="start",
    )(side[None], *far)


def mix_kernel(first, features_ref, across_ref, weights_ref, *refs):
    out_ref = refs[-1]
    mixed = jnp.dot(features_ref[...], weights_ref[first], preferred_element_type=jnp.float32)
    mixed += jnp.dot(across_ref[...], weights_ref[first + 1], preferred_element_type=jnp.float32)
    for bias_ref in refs[:-1]:
        mixed += bias_ref[...]
    out_ref[...] = mixed.astype(out_ref.dtype)


def mix(first, features, across, weights, dtype, *bias):
    whole = pl.BlockSpec(memory_space=pltpu.VMEM)
    return pl.pallas_call(
        functools.partial(mix_kernel, first),
        in_specs=[whole] * (3 + len(bias)),
        out_specs=whole,
        out_shape=pltpu.VMEM((features.shape[0], weights.shape[2]), dtype),
        compiler_params=pltpu.CompilerParams(vmem_limit_bytes=VMEM_LIMIT),
        name="mix",
    )(features, across, weights, *bias)


def load_kernel(
    parts,
    device_ref,
    spots_hbm,
    source_hbm,
    target_hbm,
    adjacency_hbm,
    tiles_ref,
    table_ref,
    spots_ref,
    source_ref,
    target_ref,
    sems,
):
    count = adjacency_hbm.shape[0]
    step = count // parts

    def copy(i):
        at = pl.ds(i * step, step)
        return pltpu.make_async_copy(adjacency_hbm.at[at], tiles_ref.at[at], sems.at[i])

    scalars = [
        pltpu.make_async_copy(spots_hbm.at[device_ref[0]], spots_ref, sems.at[parts]),
        pltpu.make_async_copy(source_hbm, source_ref, sems.at[parts + 1]),
        pltpu.make_async_copy(target_hbm, target_ref, sems.at[parts + 2]),
    ]
    for c in scalars:
        c.start()
    for i in range(parts):
        copy(i).start()
    tiles_ref[count] = jnp.zeros_like(tiles_ref[count])
    def blank(k, carry):
        table_ref[k] = count
        return carry

    lax.fori_loop(0, table_ref.shape[0], blank, 0, unroll=16)
    for c in scalars:
        c.wait()

    def add(k, carry):
        target = target_ref[k]
        source = source_ref[k]
        table_ref[spots_ref[source // TILE, source % TILE] * NTD + target] = k
        return carry

    lax.fori_loop(0, count, add, 0, unroll=8)
    for i in range(parts):
        copy(i).wait()


def degree_kernel(target_ref, tiles_ref, lanes_ref, even, odd):
    even[...] = jnp.zeros_like(even)
    odd[...] = jnp.zeros_like(odd)

    def add(k, carry):
        even[target_ref[2 * k]] += tiles_ref[2 * k].astype(jnp.float32)
        odd[target_ref[2 * k + 1]] += tiles_ref[2 * k + 1].astype(jnp.float32)
        return carry

    lax.fori_loop(0, target_ref.shape[0] // 2, add, 0, unroll=4)
    lanes_ref[...] = even[...] + odd[...]


def degree(tiles, tile_target):
    whole = pl.BlockSpec(memory_space=pltpu.VMEM)
    count = tile_target.shape[0]
    return pl.pallas_call(
        degree_kernel,
        in_specs=[pl.BlockSpec(memory_space=pltpu.SMEM), whole],
        out_specs=whole,
        out_shape=pltpu.VMEM((NTD, TILE, TILE), jnp.float32),
        scratch_shapes=[pltpu.VMEM((NTD, TILE, TILE), jnp.float32)] * 2,
        compiler_params=pltpu.CompilerParams(vmem_limit_bytes=VMEM_LIMIT),
        cost_estimate=pl.CostEstimate(
            flops=count * TILE * TILE, bytes_accessed=count * TILE * TILE * 2, transcendentals=0
        ),
        name="degree",
    )(tile_target, pltpu.with_memory_space_constraint(tiles, pltpu.VMEM))


def load(device, spots, adjacency, tile_source, tile_target):
    count = adjacency.shape[0]
    parts = 16
    there = pl.BlockSpec(memory_space=pl.ANY)
    whole = pl.BlockSpec(memory_space=pltpu.VMEM)
    scalars = pl.BlockSpec(memory_space=pltpu.SMEM)
    nodes = spots.shape[1]
    spots = jnp.asarray(spots.reshape(-1, nodes // TILE, TILE), jnp.int32)
    far = [
        pltpu.with_memory_space_constraint(x, pltpu.HBM)
        for x in (spots, tile_source, tile_target, adjacency)
    ]
    return pl.pallas_call(
        functools.partial(load_kernel, parts),
        in_specs=[scalars] + [there] * 4,
        out_specs=[whole, scalars],
        out_shape=[
            pltpu.VMEM((count + 1, TILE, TILE), adjacency.dtype),
            jax.ShapeDtypeStruct((nodes * NTD,), jnp.int32),
        ],
        scratch_shapes=[
            pltpu.SMEM((nodes // TILE, TILE), jnp.int32),
            pltpu.SMEM((count,), jnp.int32),
            pltpu.SMEM((count,), jnp.int32),
            pltpu.SemaphoreType.DMA((parts + 3,)),
        ],
        compiler_params=pltpu.CompilerParams(vmem_limit_bytes=VMEM_LIMIT),
        cost_estimate=pl.CostEstimate(
            flops=count * TILE * TILE, bytes_accessed=count * TILE * TILE * 2, transcendentals=0
        ),
        name="load",
    )(device[None], *far)


def gather_kernel(chunks, offset, first, last, table_ref, tiles_ref, *refs):
    pieces = refs[: len(chunks)]
    rest = refs[len(chunks) :]
    if last:
        total_in, lanes_ref, own_ref, out_ref, total = rest
        total[...] = total_in[...]
    elif first:
        (total,) = rest
        total[...] = jnp.zeros_like(total)
    else:
        total_in, total = rest
        total[...] = total_in[...]
    def product(piece, s, count, base):
        at = (base + s) * NTD

        def tile(t, j):
            return tiles_ref[table_ref[at + j * NTD + t]]

        left = jnp.concatenate(
            [jnp.concatenate([tile(t, j) for j in range(count)], axis=1) for t in range(NTD)],
            axis=0,
        )
        right = piece[pl.ds(pl.multiple_of(s * TILE, TILE), count * TILE)]
        return jnp.dot(left, right, preferred_element_type=jnp.float32)

    base = offset
    for piece, count in zip(pieces, chunks):

        def step(i, carry, piece=piece, base=base):
            total[...] += product(piece, i * TOGETHER, TOGETHER, base)
            return carry

        lax.fori_loop(0, count // TOGETHER, step, 0)
        if count % TOGETHER:
            total[...] += product(piece, count - count % TOGETHER, count % TOGETHER, base)
        base += count
    if last:
        degree = jnp.sum(lanes_ref[...], axis=1, keepdims=True)
        near = total[...] / jnp.sqrt(1.0 + degree)
        out_ref[...] = jnp.maximum(near + own_ref[...], 0.0).astype(out_ref.dtype)


def gathered(pieces, offset, table, tiles, width, hint, total=None, ending=None):
    tiles = pltpu.with_memory_space_constraint(tiles, pltpu.VMEM)
    chunks = [p.value.shape[0] // TILE for p in pieces]
    wide = NTD * TILE
    whole = pl.BlockSpec(memory_space=pltpu.VMEM)
    scalars = pl.BlockSpec(memory_space=pltpu.SMEM)
    extra = ([] if total is None else [total]) + ([] if ending is None else list(ending))
    count = sum(chunks)
    last = ending is not None
    return pl.pallas_call(
        functools.partial(gather_kernel, chunks, offset, total is None, last),
        in_specs=[scalars, whole] + [whole] * (len(pieces) + len(extra)),
        out_specs=whole,
        out_shape=jax.ShapeDtypeStruct((wide, width), jnp.bfloat16 if last else jnp.float32),
        scratch_shapes=[pltpu.VMEM((wide, width), jnp.float32)] if last else [],
        compiler_params=pltpu.CompilerParams(vmem_limit_bytes=VMEM_LIMIT),
        cost_estimate=pl.CostEstimate(
            flops=hint * count * TILE * wide * width,
            bytes_accessed=count * TILE * (wide + width),
            transcendentals=0,
        ),
        name="gather",
    )(table, tiles, *[p.value for p in pieces], *extra)


def body(feature_codes, group_scales, adjacency, tile_source, tile_target, weight, out_bias):
    cols = out_bias.shape[0]
    side = lax.axis_index("rep")
    device = lax.axis_index("blk") * 2 + side
    features, weights = start(side, feature_codes, group_scales, weight, cols)
    blocks = np.array([linear(c) // 2 for c in coordinates()])
    here = Piece(features, blocks[:, None] * NTD + np.arange(NTD)[None, :])
    across = moved(here, lambda y, h, x, c, z: (y, h, x, c, 1 - z))
    taken = []
    plan(Piece(None, here.tiles), lambda pieces, *_, **__: taken.extend(p.tiles for p in pieces))
    order = np.concatenate(taken, axis=1)
    spots = np.argsort(order, axis=1)
    every = np.arange(lax.axis_size("blk") * NTD)
    assert np.array_equal(np.sort(order, axis=1), np.broadcast_to(every, order.shape))
    tiles, table = load(device, spots, adjacency, tile_source, tile_target)
    near, table = lax.optimization_barrier((across.value, table))
    table, lanes = lax.optimization_barrier((table, degree(tiles, tile_target)))
    lanes = lanes.reshape(NTD * TILE, TILE)
    sent = mix(2, features, near, weights, jnp.bfloat16)
    own = mix(0, features, near, weights, jnp.float32, out_bias[None])

    total = [None]
    place = [0]

    def absorb(pieces, hint=HINT, ending=False):
        total[0] = gathered(
            pieces, place[0], table, tiles, cols, hint, total[0], (lanes, own) if ending else None
        )
        place[0] += sum(p.tiles.shape[1] for p in pieces)
        return total[0]

    plan(Piece(sent, here.tiles), absorb)
    return total[0]


def solution(mesh):
    placed = (
        P("blk", "rep"),
        P("blk", "rep"),
        P("blk", None, None),
        P("blk"),
        P("blk"),
        P(),
        P("rep"),
    )
    return jax.shard_map(
        body, mesh=mesh, in_specs=placed, out_specs=P("blk", "rep"), check_vma=False
    )
```

```python
import functools

import jax
import jax.numpy as jnp
import numpy as np
from jax import lax
from jax.experimental import pallas as pl
from jax.experimental.pallas import tpu as pltpu
from jax.sharding import PartitionSpec as P

F = 512
TILE = 128
NTD = 4
EXTENT = (4, 2, 4, 2, 2)
VMEM_LIMIT = 8 * 2**20
TOGETHER = 16
HINT = 40


def coordinates():
    return [tuple(int(v) for v in c) for c in np.ndindex(*EXTENT)]


def linear(c):
    return int(np.ravel_multi_index(tuple(v % e for v, e in zip(c, EXTENT)), EXTENT))


class Piece:
    def __init__(self, value, tiles):
        self.value = value
        self.tiles = tiles

    def rows(self, begin, end):
        value = None if self.value is None else self.value[begin * TILE : end * TILE]
        return Piece(value, self.tiles[:, begin:end])

    def halves(self):
        count = self.tiles.shape[1]
        return self.rows(0, count // 2), self.rows(count // 2, count)


def join(*pieces):
    planned = pieces[0].value is None
    return Piece(
        None if planned else jnp.concatenate([p.value for p in pieces], axis=0),
        np.concatenate([p.tiles for p in pieces], axis=1),
    )


def moved(piece, where):
    pairs = [(linear(c), linear(where(*c))) for c in coordinates()]
    tiles = np.empty_like(piece.tiles)
    for source, target in pairs:
        tiles[target] = piece.tiles[source]
    value = piece.value
    if value is not None:
        value = lax.ppermute(value, ("blk", "rep"), pairs)
    return Piece(value, tiles)


def first_axis(piece, steps):
    return moved(
        piece,
        lambda y, h, x, c, z: (y, h, x + steps, c, z) if c == 0 else (y + steps, h, x, c, z),
    )


def second_axis(piece, steps):
    return moved(
        piece,
        lambda y, h, x, c, z: (y + steps, h, x, c, z) if c == 0 else (y, h, x + steps, c, z),
    )


def over_z(piece):
    return moved(piece, lambda y, h, x, c, z: (y, h + 1, x, c, z))


def other_core(piece):
    return moved(piece, lambda y, h, x, c, z: (y, h, x, 1 - c, z))


def after(piece, others):
    if piece.value is None:
        return piece
    return Piece(lax.optimization_barrier((piece.value, *others))[0], piece.tiles)


def plan(mine, absorb):
    plus, minus, over = (first_axis(mine, s) for s in (1, -1, 2))
    z_mine = over_z(mine)
    z_pair = over_z(join(plus, minus))
    near = join(mine, plus, minus, over, z_mine)
    near_up, near_down = second_axis(near, 1), second_axis(near, -1)
    far_up = second_axis(join(z_pair, near_up.rows(0, 9)), 1)
    far_down = second_axis(join(z_pair, near_down.rows(9, 20)), -1)
    half = NTD // 2
    at = 3 * NTD
    z_over = over_z(
        after(
            join(over, near_up.rows(at, at + half), near_down.rows(at + half, at + NTD)),
            (z_pair.value,),
        )
    )
    absorb([near, other_core(near)])
    done = absorb([near_up, near_down, other_core(near_up), other_core(near_down)])
    absorb([z_pair, other_core(z_pair)])
    end_up = join(far_up.rows(0, NTD), z_over.rows(NTD, NTD + half), z_over.rows(half, NTD))
    end_down = join(far_down.rows(NTD, 2 * NTD), z_over.rows(NTD + half, 2 * NTD), z_over.rows(0, half))
    end = join(second_axis(end_up, 1), second_axis(end_down, -1))
    absorb([far_up, far_down, z_over])
    absorb([other_core(far_up), other_core(far_down), other_core(after(z_over, (done,)))])
    absorb([end, other_core(end)], ending=True)


def start_kernel(side_ref, codes_hbm, scales_hbm, weight_hbm, features_ref, weights_ref, codes_ref, scales_ref, sems):
    rows, half = codes_ref.shape
    groups = scales_ref.shape[0]
    width = half // groups
    cols = weights_ref.shape[2]
    side = side_ref[0]
    inputs = [
        pltpu.make_async_copy(codes_hbm, codes_ref, sems.at[0]),
        pltpu.make_async_copy(scales_hbm, scales_ref, sems.at[1]),
    ]
    for n in range(4):
        whose = side if n % 2 == 0 else 1 - side
        at = pl.ds(pl.multiple_of((n // 2) * F + whose * half, half), half)
        from_here = weight_hbm.at[at, pl.ds(pl.multiple_of(side * cols, cols), cols)]
        inputs.append(pltpu.make_async_copy(from_here, weights_ref.at[n], sems.at[2 + n]))
    for copy in inputs:
        copy.start()
    for copy in inputs[:2]:
        copy.wait()
    for g in range(groups):
        at = slice(g * width, (g + 1) * width)
        scales = jnp.broadcast_to(scales_ref[g : g + 1, :], (width, rows)).T
        scaled = codes_ref[:, at].astype(jnp.float32) * scales
        features_ref[:, at] = scaled.astype(features_ref.dtype)
    for copy in inputs[2:]:
        copy.wait()


def start(side, codes, scales, weight, cols):
    rows, half = codes.shape
    there = pl.BlockSpec(memory_space=pl.ANY)
    whole = pl.BlockSpec(memory_space=pltpu.VMEM)
    scales = scales.T
    far = [pltpu.with_memory_space_constraint(x, pltpu.HBM) for x in (codes, scales, weight)]
    return pl.pallas_call(
        start_kernel,
        in_specs=[pl.BlockSpec(memory_space=pltpu.SMEM)] + [there] * 3,
        out_specs=[whole, whole],
        out_shape=[pltpu.VMEM((rows, half), codes.dtype), pltpu.VMEM((4, half, cols), weight.dtype)],
        scratch_shapes=[
            pltpu.VMEM((rows, half), codes.dtype),
            pltpu.VMEM(scales.shape, scales.dtype),
            pltpu.SemaphoreType.DMA((6,)),
        ],
        compiler_params=pltpu.CompilerParams(vmem_limit_bytes=VMEM_LIMIT),
        name="start",
    )(side[None], *far)


def mix_kernel(first, features_ref, across_ref, weights_ref, *refs):
    out_ref = refs[-1]
    mixed = jnp.dot(features_ref[...], weights_ref[first], preferred_element_type=jnp.float32)
    mixed += jnp.dot(across_ref[...], weights_ref[first + 1], preferred_element_type=jnp.float32)
    for bias_ref in refs[:-1]:
        mixed += bias_ref[...]
    out_ref[...] = mixed.astype(out_ref.dtype)


def mix(first, features, across, weights, dtype, *bias):
    whole = pl.BlockSpec(memory_space=pltpu.VMEM)
    return pl.pallas_call(
        functools.partial(mix_kernel, first),
        in_specs=[whole] * (3 + len(bias)),
        out_specs=whole,
        out_shape=pltpu.VMEM((features.shape[0], weights.shape[2]), dtype),
        compiler_params=pltpu.CompilerParams(vmem_limit_bytes=VMEM_LIMIT),
        name="mix",
    )(features, across, weights, *bias)


def load_kernel(
    parts,
    device_ref,
    spots_hbm,
    source_hbm,
    target_hbm,
    adjacency_hbm,
    tiles_ref,
    table_ref,
    spots_ref,
    source_ref,
    target_ref,
    sems,
):
    count = adjacency_hbm.shape[0]
    step = count // parts

    def copy(i):
        at = pl.ds(i * step, step)
        return pltpu.make_async_copy(adjacency_hbm.at[at], tiles_ref.at[at], sems.at[i])

    scalars = [
        pltpu.make_async_copy(spots_hbm.at[device_ref[0]], spots_ref, sems.at[parts]),
        pltpu.make_async_copy(source_hbm, source_ref, sems.at[parts + 1]),
        pltpu.make_async_copy(target_hbm, target_ref, sems.at[parts + 2]),
    ]
    for c in scalars:
        c.start()
    for i in range(parts):
        copy(i).start()
    tiles_ref[count] = jnp.zeros_like(tiles_ref[count])
    def blank(k, carry):
        table_ref[k] = count
        return carry

    lax.fori_loop(0, table_ref.shape[0], blank, 0, unroll=16)
    for c in scalars:
        c.wait()

    def add(k, carry):
        target = target_ref[k]
        source = source_ref[k]
        table_ref[spots_ref[source // TILE, source % TILE] * NTD + target] = k
        return carry

    lax.fori_loop(0, count, add, 0, unroll=8)
    for i in range(parts):
        copy(i).wait()


def degree_kernel(target_ref, tiles_ref, lanes_ref, even, odd):
    even[...] = jnp.zeros_like(even)
    odd[...] = jnp.zeros_like(odd)

    def add(k, carry):
        even[target_ref[2 * k]] += tiles_ref[2 * k].astype(jnp.float32)
        odd[target_ref[2 * k + 1]] += tiles_ref[2 * k + 1].astype(jnp.float32)
        return carry

    lax.fori_loop(0, target_ref.shape[0] // 2, add, 0, unroll=4)
    lanes_ref[...] = even[...] + odd[...]


def degree(tiles, tile_target):
    whole = pl.BlockSpec(memory_space=pltpu.VMEM)
    count = tile_target.shape[0]
    return pl.pallas_call(
        degree_kernel,
        in_specs=[pl.BlockSpec(memory_space=pltpu.SMEM), whole],
        out_specs=whole,
        out_shape=pltpu.VMEM((NTD, TILE, TILE), jnp.float32),
        scratch_shapes=[pltpu.VMEM((NTD, TILE, TILE), jnp.float32)] * 2,
        compiler_params=pltpu.CompilerParams(vmem_limit_bytes=VMEM_LIMIT),
        cost_estimate=pl.CostEstimate(
            flops=count * TILE * TILE, bytes_accessed=count * TILE * TILE * 2, transcendentals=0
        ),
        name="degree",
    )(tile_target, pltpu.with_memory_space_constraint(tiles, pltpu.VMEM))


def load(device, spots, adjacency, tile_source, tile_target):
    count = adjacency.shape[0]
    parts = 16
    there = pl.BlockSpec(memory_space=pl.ANY)
    whole = pl.BlockSpec(memory_space=pltpu.VMEM)
    scalars = pl.BlockSpec(memory_space=pltpu.SMEM)
    nodes = spots.shape[1]
    spots = jnp.asarray(spots.reshape(-1, nodes // TILE, TILE), jnp.int32)
    far = [
        pltpu.with_memory_space_constraint(x, pltpu.HBM)
        for x in (spots, tile_source, tile_target, adjacency)
    ]
    return pl.pallas_call(
        functools.partial(load_kernel, parts),
        in_specs=[scalars] + [there] * 4,
        out_specs=[whole, scalars],
        out_shape=[
            pltpu.VMEM((count + 1, TILE, TILE), adjacency.dtype),
            jax.ShapeDtypeStruct((nodes * NTD,), jnp.int32),
        ],
        scratch_shapes=[
            pltpu.SMEM((nodes // TILE, TILE), jnp.int32),
            pltpu.SMEM((count,), jnp.int32),
            pltpu.SMEM((count,), jnp.int32),
            pltpu.SemaphoreType.DMA((parts + 3,)),
        ],
        compiler_params=pltpu.CompilerParams(vmem_limit_bytes=VMEM_LIMIT),
        cost_estimate=pl.CostEstimate(
            flops=count * TILE * TILE, bytes_accessed=count * TILE * TILE * 2, transcendentals=0
        ),
        name="load",
    )(device[None], *far)


def gather_kernel(chunks, offset, first, last, table_ref, tiles_ref, *refs):
    pieces = refs[: len(chunks)]
    rest = refs[len(chunks) :]
    if last:
        total_in, lanes_ref, own_ref, out_ref, total = rest
        total[...] = total_in[...]
    elif first:
        (total,) = rest
        total[...] = jnp.zeros_like(total)
    else:
        total_in, total = rest
        total[...] = total_in[...]
    def product(piece, s, count, base):
        at = (base + s) * NTD

        def tile(t, j):
            return tiles_ref[table_ref[at + j * NTD + t]]

        left = jnp.concatenate(
            [jnp.concatenate([tile(t, j) for j in range(count)], axis=1) for t in range(NTD)],
            axis=0,
        )
        right = piece[pl.ds(pl.multiple_of(s * TILE, TILE), count * TILE)]
        return jnp.dot(left, right, preferred_element_type=jnp.float32)

    base = offset
    for piece, count in zip(pieces, chunks):

        def step(i, carry, piece=piece, base=base):
            total[...] += product(piece, i * TOGETHER, TOGETHER, base)
            return carry

        lax.fori_loop(0, count // TOGETHER, step, 0)
        if count % TOGETHER:
            total[...] += product(piece, count - count % TOGETHER, count % TOGETHER, base)
        base += count
    if last:
        degree = jnp.sum(lanes_ref[...], axis=1, keepdims=True)
        near = total[...] / jnp.sqrt(1.0 + degree)
        out_ref[...] = jnp.maximum(near + own_ref[...], 0.0).astype(out_ref.dtype)


def gathered(pieces, offset, table, tiles, width, hint, total=None, ending=None):
    tiles = pltpu.with_memory_space_constraint(tiles, pltpu.VMEM)
    chunks = [p.value.shape[0] // TILE for p in pieces]
    wide = NTD * TILE
    whole = pl.BlockSpec(memory_space=pltpu.VMEM)
    scalars = pl.BlockSpec(memory_space=pltpu.SMEM)
    extra = ([] if total is None else [total]) + ([] if ending is None else list(ending))
    count = sum(chunks)
    last = ending is not None
    return pl.pallas_call(
        functools.partial(gather_kernel, chunks, offset, total is None, last),
        in_specs=[scalars, whole] + [whole] * (len(pieces) + len(extra)),
        out_specs=whole,
        out_shape=jax.ShapeDtypeStruct((wide, width), jnp.bfloat16 if last else jnp.float32),
        scratch_shapes=[pltpu.VMEM((wide, width), jnp.float32)] if last else [],
        compiler_params=pltpu.CompilerParams(vmem_limit_bytes=VMEM_LIMIT),
        cost_estimate=pl.CostEstimate(
            flops=hint * count * TILE * wide * width,
            bytes_accessed=count * TILE * (wide + width),
            transcendentals=0,
        ),
        name="gather",
    )(table, tiles, *[p.value for p in pieces], *extra)


def body(feature_codes, group_scales, adjacency, tile_source, tile_target, weight, out_bias):
    cols = out_bias.shape[0]
    side = lax.axis_index("rep")
    device = lax.axis_index("blk") * 2 + side
    features, weights = start(side, feature_codes, group_scales, weight, cols)
    blocks = np.array([linear(c) // 2 for c in coordinates()])
    here = Piece(features, blocks[:, None] * NTD + np.arange(NTD)[None, :])
    across = moved(here, lambda y, h, x, c, z: (y, h, x, c, 1 - z))
    taken = []
    plan(Piece(None, here.tiles), lambda pieces, *_, **__: taken.extend(p.tiles for p in pieces))
    order = np.concatenate(taken, axis=1)
    spots = np.argsort(order, axis=1)
    every = np.arange(lax.axis_size("blk") * NTD)
    assert np.array_equal(np.sort(order, axis=1), np.broadcast_to(every, order.shape))
    tiles, table = load(device, spots, adjacency, tile_source, tile_target)
    near, table = lax.optimization_barrier((across.value, table))
    table, lanes = lax.optimization_barrier((table, degree(tiles, tile_target)))
    lanes = lanes.reshape(NTD * TILE, TILE)
    sent = mix(2, features, near, weights, jnp.bfloat16)
    own = mix(0, features, near, weights, jnp.float32, out_bias[None])

    total = [None]
    place = [0]

    def absorb(pieces, hint=HINT, ending=False):
        total[0] = gathered(
            pieces, place[0], table, tiles, cols, hint, total[0], (lanes, own) if ending else None
        )
        place[0] += sum(p.tiles.shape[1] for p in pieces)
        return total[0]

    plan(Piece(sent, here.tiles), absorb)
    return total[0]


def solution(mesh):
    placed = (
        P("blk", "rep"),
        P("blk", "rep"),
        P("blk", None, None),
        P("blk"),
        P("blk"),
        P(),
        P("rep"),
    )
    return jax.shard_map(
        body, mesh=mesh, in_specs=placed, out_specs=P("blk", "rep"), check_vma=False
    )
```
